32 devices in a mesh: row: 4 (over z), col: 8 (over y, x, core).
Axes of the slice: x: 2, y: 2, z: 4, core: 2. Of those that a mesh axis runs over, the one named last changes fastest.
Arguments:
- panel_first: bfloat16 [32, 256, 1024], P(('row', 'col')), may hold values from -3 to 3
- panel_second: bfloat16 [32, 256, 1024], P(('row', 'col')), may hold values from -4 to 4
- diag_first: bfloat16 [1024, 1024], P('col'), as said below
- bridge: bfloat16 [1024, 1024], P('col'), may hold values from -0.024902344 to 0.024902344
- diag_second: bfloat16 [1024, 1024], P('col'), as said below
- trailing: float32 [32, 24, 256, 256], P(('row', 'col')), may hold values from -6 to 6
- trail_pairs: int32 [32, 2, 24], P(('row', 'col')), may hold values from 0 to 7, as said below
- live_count: int32 [32], P(('row', 'col')), may hold values from 1 to 24, as said below
Outputs:
- lower_first: bfloat16 [32, 256, 1024], P(('row', 'col'))
- lower_second: bfloat16 [32, 256, 1024], P(('row', 'col'))
- trailing_out: float32 [32, 24, 256, 256], P(('row', 'col'))
The draws below stay inside these ranges and needn't reach their ends.
Inputs may be any that keep to these rules, and one draw needn't show every extreme that they name: `trail_pairs`: on each device the listed pairs are distinct; the first entry of a pair is below 8 and the second below 4. `live_count`: some device has all 24 slots live in every draw. `diag_first`: symmetric and positive definite, with diagonal entries between 0.75 and 2.3. `diag_second`: symmetric and positive definite, with diagonal entries between 3.4 and 7.5.
All inputs are finite; a program needn't handle non-finite values.
Results may differ from the reference program's by a relative error of at most 0.001.
Values may be sent and summed in bfloat16 or wider, within the bound.
A program may use at most 192 MiB of HBM per device.

```python
import jax
import jax.numpy as jnp
from jax import lax

PANEL = 1024
TILE = 256
SLOTS = 24
PTILES = 32
N_ROW = 4
N_COL = 8


def definite_block(base_key, low_diag, high_diag, unit_part, low_load, high_load, rough_total):
    rough_key, scale_key, load_key = jax.random.split(base_key, 3)
    group = max(PANEL // 16, 1)
    limit = rough_total / (PANEL - 1)
    raw = jax.random.uniform(rough_key, (PANEL, PANEL), jnp.float32, -limit, limit)
    upper = jnp.triu(raw, 1)
    rough = upper + upper.T
    load = jax.random.uniform(load_key, (PANEL,), jnp.float32, low_load, high_load)
    member = jnp.arange(PANEL) // group
    same = member[:, None] == member[None, :]
    shared = jnp.where(same, load[:, None] * load[None, :], 0.0)
    core = rough + shared + unit_part * jnp.eye(PANEL, dtype=jnp.float32)
    scale = jax.random.uniform(scale_key, (PANEL,), jnp.float32, low_diag, high_diag)
    root = jnp.sqrt(scale)
    outer = root[:, None] * root[None, :]
    return (outer * core).astype(jnp.bfloat16)


def draw_diag_first(key, part):
    return definite_block(jax.random.fold_in(key, 11), 1.0, 2.0, 0.5, 0.5, 0.8, 0.15)


def draw_diag_second(key, part):
    return definite_block(jax.random.fold_in(key, 12), 3.0, 5.0, 1.0, 0.4, 0.7, 0.3)


def draw_bridge(key, part):
    values = jax.random.uniform(jax.random.fold_in(key, 15), (PANEL, PANEL), jnp.float32, -0.026, 0.026)
    values = jnp.clip(values, -0.02490234375, 0.02490234375)
    return values.astype(jnp.bfloat16)


def draw_trail_pairs(key, part):
    key_list = jax.random.split(jax.random.fold_in(key, 13), PTILES)

    def one_list(single_key):
        shuffled = jax.random.permutation(single_key, N_ROW * N_COL)[:SLOTS]
        return jnp.stack([shuffled // N_ROW, shuffled % N_ROW]).astype(jnp.int32)
    return jax.vmap(one_list)(key_list)


def draw_live_count(key, part):
    base_key, heavy_key, pick_key = jax.random.split(jax.random.fold_in(key, 14), 3)
    modest = jax.random.randint(base_key, (PTILES,), 1, SLOTS // 2 + 1)
    heavy = jax.random.randint(heavy_key, (PTILES,), 0, 8) == 0
    chosen = jax.random.randint(pick_key, (), 0, PTILES)
    loaded = heavy | (jnp.arange(PTILES) == chosen)
    return jnp.where(loaded, SLOTS, modest).astype(jnp.int32)


def levels(stream_key, shape, shards, smallest, top_value):
    gain, own = 1.0, jax.random.fold_in(stream_key, 6)
    for axis_at, shards_of in shards:
        draws = jnp.exp(jax.random.uniform(jax.random.fold_in(own, axis_at), (shards_of,), jnp.float32, smallest / len(shards), top_value / len(shards)))
        gain = gain * jnp.repeat(draws, shape[axis_at] // shards_of).reshape([-1 if axis == axis_at else 1 for axis in range(len(shape))])
    return gain


def normal_values(stream_key, shape, width, bound, shards=(), held_as=jnp.bfloat16):
    drawn = width * jax.random.normal(stream_key, shape, jnp.float32)
    if shards:
        drawn = drawn * levels(stream_key, shape, shards, -0.22, 0.18)
    return jnp.clip(drawn, -bound, bound).astype(held_as)


def setup_inputs(seed: int = 0) -> dict:
    key_of = jax.random.split(jax.random.key(seed), 9)
    return {
        "panel_first": normal_values(key_of[0], (PTILES, TILE, PANEL), 0.2, 3.0, ((0, 32),)),
        "panel_second": normal_values(key_of[1], (PTILES, TILE, PANEL), 0.3, 4.0, ((0, 32),)),
        "diag_first": draw_diag_first(jax.random.fold_in(key_of[8], 71), 0),
        "bridge": draw_bridge(jax.random.fold_in(key_of[8], 71), 0),
        "diag_second": draw_diag_second(jax.random.fold_in(key_of[8], 71), 0),
        "trailing": normal_values(key_of[5], (PTILES, SLOTS, TILE, TILE), 1.0, 6.0, ((0, 32),), jnp.float32),
        "trail_pairs": draw_trail_pairs(jax.random.fold_in(key_of[8], 71), 0),
        "live_count": draw_live_count(jax.random.fold_in(key_of[8], 71), 0),
    }


def right_solve(lower_factor, block_rows):
    return jax.scipy.linalg.solve_triangular(lower_factor, block_rows.T, lower=True).T

def reference(panel_first, panel_second, diag_first, bridge, diag_second, trailing, trail_pairs, live_count):
    highest = lax.Precision.HIGHEST
    factor_first = jnp.linalg.cholesky(diag_first.astype(jnp.float32))
    coupling = right_solve(factor_first, bridge.astype(jnp.float32))
    shifted = diag_second.astype(jnp.float32) - jnp.dot(coupling.astype(jnp.float32), coupling.T.astype(jnp.float32), precision=highest, preferred_element_type=jnp.float32)
    factor_second = jnp.linalg.cholesky(shifted)
    flat_first = panel_first.astype(jnp.float32).reshape(PTILES * TILE, PANEL)
    lower_first = right_solve(factor_first, flat_first).astype(jnp.bfloat16)
    flat_second = panel_second.astype(jnp.float32).reshape(PTILES * TILE, PANEL)
    reduced = flat_second - jnp.dot(lower_first.astype(jnp.float32), coupling.T.astype(jnp.float32), precision=highest, preferred_element_type=jnp.float32)
    lower_second = right_solve(factor_second, reduced).astype(jnp.bfloat16)
    lower_first = lower_first.reshape(PTILES, TILE, PANEL)
    lower_second = lower_second.reshape(PTILES, TILE, PANEL)
    stacked = jnp.concatenate([lower_first, lower_second], axis=2).astype(jnp.float32)

    def one_device(packed):
        device_index, tiles_in, pair_list, live_slots = packed
        grid_row = device_index // N_COL
        grid_col = device_index % N_COL
        left_tiles = stacked[(grid_row * N_COL + pair_list[0]).astype(jnp.int32)]
        right_tiles = stacked[(pair_list[1] * N_COL + grid_col).astype(jnp.int32)]
        products = jnp.einsum('sik,sjk->sij', left_tiles, right_tiles, precision=highest)
        active = (jnp.arange(SLOTS, dtype=jnp.int32) < live_slots)[:, None, None]
        return tiles_in - jnp.where(active, products, jnp.zeros_like(products))
    trailing_out = lax.map(one_device, (jnp.arange(PTILES, dtype=jnp.int32), trailing, trail_pairs, live_count))
    return (lower_first, lower_second, trailing_out)
```

```python
import functools

import jax
import jax.numpy as jnp
from jax import lax
from jax.experimental import pallas as pl
from jax.experimental.pallas import tpu as pltpu
from jax.sharding import PartitionSpec as P

BLOCK = 128
MICRO = 16
HALF = 8
F32 = jnp.float32
BF16 = jnp.bfloat16


def split_outside(x):
    high = lax.reduce_precision(x, 8, 7)
    return high.astype(BF16), (x - high).astype(BF16)


def split2(x):
    high = x.astype(BF16)
    return high, (x - high.astype(F32)).astype(BF16)


def split3(x):
    high = x.astype(BF16)
    rest = x - high.astype(F32)
    mid = rest.astype(BF16)
    return high, mid, (rest - mid.astype(F32)).astype(BF16)


def dot_tn(left, right):
    return lax.dot_general(left, right, (((0,), (0,)), ((), ())), preferred_element_type=F32)


def dot_nn(left, right):
    return lax.dot_general(left, right, (((1,), (0,)), ((), ())), preferred_element_type=F32)


def dot_nt(left, right):
    return lax.dot_general(left, right, (((1,), (1,)), ((), ())), preferred_element_type=F32)


def inverse_factor_block(block):
    rows = lax.broadcasted_iota(jnp.int32, (HALF, BLOCK), 0)
    row = lax.broadcasted_iota(jnp.int32, (BLOCK, BLOCK), 0)
    column = lax.broadcasted_iota(jnp.int32, (BLOCK, BLOCK), 1)
    left = block
    right = jnp.where(row == column, 1.0, 0.0).astype(F32)
    done = []
    for first in range(0, BLOCK, MICRO):
        last = first + MICRO
        here = left[:MICRO]
        pieces = [
            [here[h : h + HALF] for h in range(0, MICRO, HALF)],
            [right[h : h + HALF] for h in range(0, MICRO, HALF)],
        ]
        columns = [
            [
                jnp.broadcast_to(piece[:, first + k : first + k + 1], (HALF, BLOCK))
                for piece in pieces[0]
            ]
            for k in range(MICRO)
        ]
        pivots = [jnp.ones((HALF, BLOCK), F32) for _ in range(MICRO // HALF)]
        for i in range(MICRO):
            part, within = divmod(i, HALF)
            pivot = jnp.broadcast_to(columns[i][part][within : within + 1], (HALF, BLOCK))
            pivots[part] = jnp.where(rows == within, pivot, pivots[part])
            inverse = 1.0 / pivot
            factors = {}
            for other in range(part, MICRO // HALF):
                below = columns[i][other]
                if other == part:
                    below = jnp.where(rows > within, below, 0.0)
                factors[other] = below * inverse
            for held in pieces + columns[i + 1 :]:
                source = jnp.broadcast_to(held[part][within : within + 1], (HALF, BLOCK))
                for other in range(part, MICRO // HALF):
                    held[other] = held[other] - factors[other] * source
        scales = [lax.rsqrt(pivot) for pivot in pivots]
        upper = jnp.concatenate([a * s for a, s in zip(pieces[0], scales)], axis=0)
        inner = jnp.concatenate([a * s for a, s in zip(pieces[1], scales)], axis=0)
        done.append(inner)
        if last < BLOCK:
            uh, um, ul = split3(upper)
            wh, wm, wl = split3(inner)
            lhs = jnp.concatenate([uh, uh, um, um, uh, ul], axis=0)
            rhs_u = jnp.concatenate([uh, um, uh, um, ul, uh], axis=0)
            rhs_w = jnp.concatenate([wh, wm, wh, wm, wl, wh], axis=0)
            update_u = dot_tn(lhs, rhs_u)
            update_w = dot_tn(lhs, rhs_w)
            left = left[MICRO:] - update_u[last:]
            right = right[MICRO:] - update_w[last:]
    return jnp.concatenate(done, axis=0)


def factor_kernel(a_ref, high_ref, low_ref, grid_ref, terms_ref, flipped_ref):
    size = a_ref.shape[0]
    blocks = size // BLOCK
    grid_ref[...] = a_ref[...].astype(F32)

    @pl.loop(0, blocks)
    def _(k):
        here = pl.ds(pl.multiple_of(k * BLOCK, BLOCK), BLOCK)
        inverse = inverse_factor_block(grid_ref[here, here])
        grid_ref[here, here] = jnp.zeros((BLOCK, BLOCK), F32)
        inv_h, inv_l = split2(inverse)
        line_h, line_l = split2(grid_ref[here, :])
        grid_ref[here, :] = dot_nn(
            jnp.concatenate([inv_h, inv_h, inv_l], axis=1),
            jnp.concatenate([line_h, line_l, line_h], axis=0),
        )
        grid_ref[here, here] = inverse
        line_h, line_l = split2(grid_ref[here, :])
        terms_ref[...] = jnp.concatenate([line_h, line_l, line_h], axis=0)
        flipped_ref[...] = jnp.concatenate([line_h, line_h, line_l], axis=0)

        @pl.loop(k + 1, blocks)
        def _(i):
            below = pl.ds(pl.multiple_of(i * BLOCK, BLOCK), BLOCK)
            grid_ref[below, here] = jnp.zeros((BLOCK, BLOCK), F32)
            grid_ref[below, :] -= dot_tn(flipped_ref[:, below], terms_ref[...])

        column = lax.broadcasted_iota(jnp.int32, (BLOCK, size), 1)
        final = jnp.where(column < (k + 1) * BLOCK, grid_ref[here, :], 0.0)
        final_h, final_l = split2(final)
        high_ref[here, :] = final_h
        low_ref[here, :] = final_l


def inverse_factor(block):
    size = block.shape[0]
    whole = pl.BlockSpec(memory_space=pltpu.VMEM)
    return pl.pallas_call(
        factor_kernel,
        out_shape=[jax.ShapeDtypeStruct((size, size), BF16)] * 2,
        in_specs=[whole],
        out_specs=[whole, whole],
        scratch_shapes=[
            pltpu.VMEM((size, size), F32),
            pltpu.VMEM((3 * BLOCK, size), BF16),
            pltpu.VMEM((3 * BLOCK, size), BF16),
        ],
        compiler_params=pltpu.CompilerParams(vmem_limit_bytes=40 * 2**20),
        cost_estimate=pl.CostEstimate(flops=60 * 10**9, bytes_accessed=8 * 2**20, transcendentals=0),
        name="inverse_factor",
    )(block)


def trailing_kernel(pairs_ref, live_ref, row1_ref, row2_ref, col1_ref, col2_ref, in_ref, out_ref):
    slot = pl.program_id(0)

    @pl.when(slot < live_ref[0])
    def _():
        a = pairs_ref[0, slot]
        b = pairs_ref[1, slot]
        out_ref[0] = (
            in_ref[0] - dot_nt(row1_ref[a], col1_ref[b]) - dot_nt(row2_ref[a], col2_ref[b])
        )

    @pl.when(slot >= live_ref[0])
    def _():
        out_ref[0] = in_ref[0]


def trailing_update(pairs, live, row1, row2, col1, col2, trailing):
    slots, tile, _ = trailing.shape
    panel = row1.shape[-1]

    def whole(array):
        return pl.BlockSpec(array.shape, lambda s, *_: (0, 0, 0), pipeline_mode=pl.Buffered(1))

    one = pl.BlockSpec((1, tile, tile), lambda s, *_: (s, 0, 0))
    return pl.pallas_call(
        trailing_kernel,
        out_shape=jax.ShapeDtypeStruct(trailing.shape, F32),
        grid_spec=pltpu.PrefetchScalarGridSpec(
            num_scalar_prefetch=2,
            grid=(slots,),
            in_specs=[whole(row1), whole(row2), whole(col1), whole(col2), one],
            out_specs=one,
        ),
        compiler_params=pltpu.CompilerParams(vmem_limit_bytes=56 * 2**20),
        cost_estimate=pl.CostEstimate(
            flops=4 * slots * tile * tile * panel, bytes_accessed=30 * 2**20, transcendentals=0
        ),
        name="trailing_update",
    )(pairs, live, row1, row2, col1, col2, trailing)


def per_device(
    panel_first, panel_second, diag_first, bridge, diag_second, trailing, trail_pairs, live_count
):
    whole_first = lax.all_gather(diag_first, "col", axis=0, tiled=True)
    whole_bridge = lax.all_gather(bridge, "col", axis=0, tiled=True)
    whole_second = lax.all_gather(diag_second, "col", axis=0, tiled=True)

    first_h, first_l = inverse_factor(whole_first)
    lower_first = (dot_nt(panel_first[0], first_h) + dot_nt(panel_first[0], first_l)).astype(BF16)
    row_first = lax.all_gather(lower_first, "col", axis=0)
    col_first = lax.all_gather(lower_first, "row", axis=0)
    coupling = dot_nt(whole_bridge, first_h) + dot_nt(whole_bridge, first_l)
    c_high, c_low = split_outside(coupling)
    cross = dot_nt(c_high, c_low)
    shifted = whole_second.astype(F32) - (dot_nt(c_high, c_high) + cross + cross.T)
    second_h, second_l = inverse_factor(shifted)
    reduced = panel_second[0].astype(F32) - (dot_nt(lower_first, c_high) + dot_nt(lower_first, c_low))
    r_high, r_low = split_outside(reduced)
    lower_second = (
        dot_nt(r_high, second_h) + dot_nt(r_high, second_l) + dot_nt(r_low, second_h)
    ).astype(BF16)
    row_second = lax.all_gather(lower_second, "col", axis=0)
    col_second = lax.all_gather(lower_second, "row", axis=0)
    owned = trailing_update(
        trail_pairs[0], live_count, row_first, row_second, col_first, col_second, trailing[0]
    )
    return (lower_first[None], lower_second[None], owned[None])


def solution(mesh):
    return jax.shard_map(
        per_device,
        mesh=mesh,
        in_specs=(
            P(("row", "col"), None, None),
            P(("row", "col"), None, None),
            P("col", None),
            P("col", None),
            P("col", None),
            P(("row", "col"), None, None, None),
            P(("row", "col"), None, None),
            P(("row", "col")),
        ),
        out_specs=(
            P(("row", "col"), None, None),
            P(("row", "col"), None, None),
            P(("row", "col"), None, None, None),
        ),
        check_vma=False,
    )
```

```python
import functools

import jax
import jax.numpy as jnp
from jax import lax
from jax.experimental import pallas as pl
from jax.experimental.pallas import tpu as pltpu
from jax.sharding import PartitionSpec as P

BLOCK = 128
MICRO = 16
HALF = 8
CHUNK = 256
F32 = jnp.float32
BF16 = jnp.bfloat16


def split2(x):
    high = x.astype(BF16)
    return high, (x - high.astype(F32)).astype(BF16)


def split3(x):
    high = x.astype(BF16)
    rest = x - high.astype(F32)
    mid = rest.astype(BF16)
    return high, mid, (rest - mid.astype(F32)).astype(BF16)


def dot_tn(left, right):
    return lax.dot_general(left, right, (((0,), (0,)), ((), ())), preferred_element_type=F32)


def dot_nn(left, right):
    return lax.dot_general(left, right, (((1,), (0,)), ((), ())), preferred_element_type=F32)


def dot_nt(left, right):
    return lax.dot_general(left, right, (((1,), (1,)), ((), ())), preferred_element_type=F32)


def inverse_factor_block(block):
    rows = lax.broadcasted_iota(jnp.int32, (HALF, BLOCK), 0)
    row = lax.broadcasted_iota(jnp.int32, (BLOCK, BLOCK), 0)
    column = lax.broadcasted_iota(jnp.int32, (BLOCK, BLOCK), 1)
    left = block
    right = jnp.where(row == column, 1.0, 0.0).astype(F32)
    done = []
    for first in range(0, BLOCK, MICRO):
        last = first + MICRO
        here = left[:MICRO]
        pieces = [
            [here[h : h + HALF] for h in range(0, MICRO, HALF)],
            [right[h : h + HALF] for h in range(0, MICRO, HALF)],
        ]
        columns = [
            [
                jnp.broadcast_to(piece[:, first + k : first + k + 1], (HALF, BLOCK))
                for piece in pieces[0]
            ]
            for k in range(MICRO)
        ]
        pivots = [jnp.ones((HALF, BLOCK), F32) for _ in range(MICRO // HALF)]
        for i in range(MICRO):
            part, within = divmod(i, HALF)
            pivot = jnp.broadcast_to(columns[i][part][within : within + 1], (HALF, BLOCK))
            pivots[part] = jnp.where(rows == within, pivot, pivots[part])
            inverse = 1.0 / pivot
            factors = {}
            for other in range(part, MICRO // HALF):
                below = columns[i][other]
                if other == part:
                    below = jnp.where(rows > within, below, 0.0)
                factors[other] = below * inverse
            for held in pieces + columns[i + 1 :]:
                source = jnp.broadcast_to(held[part][within : within + 1], (HALF, BLOCK))
                for other in range(part, MICRO // HALF):
                    held[other] = held[other] - factors[other] * source
        scales = [lax.rsqrt(pivot) for pivot in pivots]
        upper = jnp.concatenate([a * s for a, s in zip(pieces[0], scales)], axis=0)
        inner = jnp.concatenate([a * s for a, s in zip(pieces[1], scales)], axis=0)
        done.append(inner)
        if last < BLOCK:
            uh, um, ul = split3(upper)
            wh, wm, wl = split3(inner)
            lhs = jnp.concatenate([uh, uh, um, um, uh, ul], axis=0)
            rhs_u = jnp.concatenate([uh, um, uh, um, ul, uh], axis=0)
            rhs_w = jnp.concatenate([wh, wm, wh, wm, wl, wh], axis=0)
            update_u = dot_tn(lhs, rhs_u)
            update_w = dot_tn(lhs, rhs_w)
            left = left[MICRO:] - update_u[last:]
            right = right[MICRO:] - update_w[last:]
    return jnp.concatenate(done, axis=0)


def run_factor(high_ref, low_ref, grid_ref, terms_ref, flipped_ref):
    size = grid_ref.shape[0]
    blocks = size // BLOCK

    @pl.loop(0, blocks)
    def _(k):
        here = pl.ds(pl.multiple_of(k * BLOCK, BLOCK), BLOCK)
        inverse = inverse_factor_block(grid_ref[here, here])
        grid_ref[here, here] = jnp.zeros((BLOCK, BLOCK), F32)
        inv_h, inv_l = split2(inverse)
        line_h, line_l = split2(grid_ref[here, :])
        grid_ref[here, :] = dot_nn(
            jnp.concatenate([inv_h, inv_h, inv_l], axis=1),
            jnp.concatenate([line_h, line_l, line_h], axis=0),
        )
        grid_ref[here, here] = inverse
        line_h, line_l = split2(grid_ref[here, :])
        terms_ref[...] = jnp.concatenate([line_h, line_l, line_h], axis=0)
        flipped_ref[...] = jnp.concatenate([line_h, line_h, line_l], axis=0)

        @pl.loop(k + 1, blocks)
        def _(i):
            below = pl.ds(pl.multiple_of(i * BLOCK, BLOCK), BLOCK)
            grid_ref[below, here] = jnp.zeros((BLOCK, BLOCK), F32)
            grid_ref[below, :] -= dot_tn(flipped_ref[:, below], terms_ref[...])

        column = lax.broadcasted_iota(jnp.int32, (BLOCK, size), 1)
        final = jnp.where(column < (k + 1) * BLOCK, grid_ref[here, :], 0.0)
        final_h, final_l = split2(final)
        high_ref[here, :] = final_h
        low_ref[here, :] = final_l


def first_kernel(a_ref, *refs):
    high_ref, low_ref, grid_ref, terms_ref, flipped_ref = refs[-5:]
    grid_ref[...] = a_ref[...].astype(F32)
    run_factor(high_ref, low_ref, grid_ref, terms_ref, flipped_ref)


def second_kernel(bridge_ref, fh_ref, fl_ref, d_ref, *refs):
    ch_ref, cl_ref, high_ref, low_ref, grid_ref, terms_ref, flipped_ref = refs[-7:]
    size = d_ref.shape[0]

    @pl.loop(0, size // CHUNK)
    def _(i):
        rows = pl.ds(pl.multiple_of(i * CHUNK, CHUNK), CHUNK)
        for first in range(0, size, CHUNK):
            last = first + CHUNK
            part = bridge_ref[rows, :last]
            value = dot_nt(part, fh_ref[first:last, :last]) + dot_nt(part, fl_ref[first:last, :last])
            ch_ref[rows, first:last], cl_ref[rows, first:last] = split2(value)

    @pl.loop(0, size // CHUNK)
    def _(i):
        rows = pl.ds(pl.multiple_of(i * CHUNK, CHUNK), CHUNK)
        part_h, part_l = ch_ref[rows, :], cl_ref[rows, :]
        for first in range(0, size, CHUNK):
            last = first + CHUNK
            other_h, other_l = ch_ref[first:last, :], cl_ref[first:last, :]
            product = dot_nt(part_h, other_h) + (dot_nt(part_h, other_l) + dot_nt(part_l, other_h))
            grid_ref[rows, first:last] = d_ref[rows, first:last].astype(F32) - product

    run_factor(high_ref, low_ref, grid_ref, terms_ref, flipped_ref)


def factor_call(kernel, outs, name, operands, arrived):
    size = operands[0].shape[0]
    whole = pl.BlockSpec(memory_space=pltpu.VMEM)
    return pl.pallas_call(
        kernel,
        out_shape=[jax.ShapeDtypeStruct((size, size), BF16)] * outs,
        in_specs=[whole] * len(operands) + [pl.BlockSpec(memory_space=pl.ANY)] * len(arrived),
        out_specs=[whole] * outs,
        scratch_shapes=[
            pltpu.VMEM((size, size), F32),
            pltpu.VMEM((3 * BLOCK, size), BF16),
            pltpu.VMEM((3 * BLOCK, size), BF16),
        ],
        compiler_params=pltpu.CompilerParams(vmem_limit_bytes=48 * 2**20),
        cost_estimate=pl.CostEstimate(flops=60 * 10**9, bytes_accessed=8 * 2**20, transcendentals=0),
        name=name,
    )(*operands, *arrived)


def solve_kernel(tile_ref, high_ref, low_ref, second_ref, *refs):
    lower_ref, again_ref = refs[-2:]
    panel = tile_ref.shape[1]
    for first in range(0, panel, CHUNK):
        last = first + CHUNK
        part = tile_ref[:, :last]
        value = dot_nt(part, high_ref[first:last, :last]) + dot_nt(part, low_ref[first:last, :last])
        lower_ref[:, first:last] = value.astype(BF16)
    again_ref[...] = second_ref[...]


def first_solve(tile, high, low, second, arrived):
    whole = pl.BlockSpec(memory_space=pltpu.VMEM)
    return pl.pallas_call(
        solve_kernel,
        out_shape=[jax.ShapeDtypeStruct(tile.shape, BF16)] * 2,
        in_specs=[whole] * 4 + [pl.BlockSpec(memory_space=pl.ANY)] * len(arrived),
        out_specs=[whole] * 2,
        compiler_params=pltpu.CompilerParams(vmem_limit_bytes=32 * 2**20),
        name="first_solve",
    )(tile, high, low, second, *arrived)


def finish_kernel(tiles, n_col, pairs_ref, live_ref, origin_ref, ch_ref, cl_ref, wh_ref, wl_ref, *refs):
    gathered, seconds, firsts = refs[0], refs[1 : 1 + tiles], refs[1 + tiles : 1 + 2 * tiles - n_col]
    in_ref, lower_ref, out_ref, x_ref, y_ref, rh_ref, rl_ref, sems = refs[-8:]
    slot = pl.program_id(0)
    panel = x_ref.shape[-1]

    @pl.when(slot == 0)
    def _():
        copies = []
        for t in range(tiles):
            source = gathered.at[origin_ref[t]] if t < n_col else firsts[t - n_col]
            copies.append(pltpu.make_async_copy(source, x_ref.at[t], sems.at[0, t]))
            copies.append(pltpu.make_async_copy(seconds[t], y_ref.at[t], sems.at[1, t]))
        for copy in copies:
            copy.start()
        for copy in copies:
            copy.wait()

        @pl.loop(0, tiles)
        def _(t):
            lower = x_ref[t]
            for first in range(0, panel, CHUNK):
                part = slice(first, first + CHUNK)
                reduced = y_ref[t, :, part].astype(F32) - (
                    dot_nt(lower, ch_ref[part, :]) + dot_nt(lower, cl_ref[part, :])
                )
                rh_ref[:, part], rl_ref[:, part] = split2(reduced)
            for first in range(0, panel, CHUNK):
                last = first + CHUNK
                high, low = rh_ref[:, :last], rl_ref[:, :last]
                w_high, w_low = wh_ref[first:last, :last], wl_ref[first:last, :last]
                value = dot_nt(high, w_high) + (dot_nt(high, w_low) + dot_nt(low, w_high))
                y_ref[t, :, first:last] = value.astype(BF16)

        lower_ref[...] = y_ref[0]

    @pl.when(slot < live_ref[0])
    def _():
        a = pairs_ref[0, slot]
        b = pairs_ref[1, slot]
        out_ref[0] = in_ref[0] - (dot_nt(x_ref[a], x_ref[b]) + dot_nt(y_ref[a], y_ref[b]))

    @pl.when(slot >= live_ref[0])
    def _():
        out_ref[0] = in_ref[0]


def finish(pairs, live, origin, couplings, inverses, gathered, seconds, firsts, trailing):
    slots, tile, _ = trailing.shape
    n_col, _, panel = gathered.shape
    tiles = len(seconds)
    fixed = pl.BlockSpec((panel, panel), lambda s, *_: (0, 0), pipeline_mode=pl.Buffered(1))
    one = pl.BlockSpec((1, tile, tile), lambda s, *_: (s, 0, 0))
    return pl.pallas_call(
        functools.partial(finish_kernel, tiles, n_col),
        out_shape=[
            jax.ShapeDtypeStruct((tile, panel), BF16),
            jax.ShapeDtypeStruct(trailing.shape, F32),
        ],
        grid_spec=pltpu.PrefetchScalarGridSpec(
            num_scalar_prefetch=3,
            grid=(slots,),
            in_specs=[fixed] * 4 + [pl.BlockSpec(memory_space=pl.ANY)] * (1 + 2 * tiles - n_col) + [one],
            out_specs=[pl.BlockSpec((tile, panel), lambda s, *_: (0, 0)), one],
            scratch_shapes=[
                pltpu.VMEM((tiles, tile, panel), BF16),
                pltpu.VMEM((tiles, tile, panel), BF16),
                pltpu.VMEM((tile, panel), BF16),
                pltpu.VMEM((tile, panel), BF16),
                pltpu.SemaphoreType.DMA((2, tiles)),
            ],
        ),
        compiler_params=pltpu.CompilerParams(vmem_limit_bytes=56 * 2**20),
        cost_estimate=pl.CostEstimate(
            flops=4 * slots * tile * tile * panel + 10 * tiles * tile * panel * panel,
            bytes_accessed=30 * 2**20,
            transcendentals=0,
        ),
        name="solve_and_update",
    )(pairs, live, origin, *couplings, *inverses, gathered, *seconds, *firsts, trailing)


def shifted_copies(array, name, count, start=1, stop=None):
    return [
        lax.ppermute(array, name, [(i, (i + s) % count) for i in range(count)])
        for s in range(start, count if stop is None else stop)
    ]


def per_device(
    n_row, n_col,
    panel_first, panel_second, diag_first, bridge, diag_second, trailing, trail_pairs, live_count,
):
    whole_first = lax.all_gather(diag_first, "col", axis=0, tiled=True)
    whole_bridge = lax.all_gather(bridge, "col", axis=0, tiled=True)
    whole_second = lax.all_gather(diag_second, "col", axis=0, tiled=True)
    one, two = 1 + 3 * n_col // 8, 1 + 5 * n_col // 8
    early = shifted_copies(panel_second[0], "col", n_col, 1, one)
    middle = shifted_copies(panel_second[0], "col", n_col, one, two)
    second_row = shifted_copies(panel_second[0], "row", n_row)

    r, c = lax.axis_index("row"), lax.axis_index("col")
    up = (r - trail_pairs[0, 1] + n_row) % n_row
    pairs = jnp.stack(
        [(c - trail_pairs[0, 0] + n_col) % n_col, jnp.where(up == 0, 0, n_col - 1 + up)]
    )

    first_h, first_l = factor_call(first_kernel, 2, "first_factor", [whole_first], early)
    lower_first, second_again = first_solve(
        panel_first[0], first_h, first_l, panel_second[0], second_row + middle
    )
    late = shifted_copies(second_again, "col", n_col, two)
    first_col = lax.all_gather(lower_first, "col", axis=0)
    first_row = shifted_copies(lower_first, "row", n_row)
    c_high, c_low, second_h, second_l = factor_call(
        second_kernel, 4, "second_factor", [whole_bridge, first_h, first_l, whole_second], []
    )
    lower_second, owned = finish(
        pairs,
        live_count,
        (c - jnp.arange(n_col, dtype=jnp.int32) + n_col) % n_col,
        (c_high, c_low),
        (second_h, second_l),
        first_col,
        [panel_second[0]] + early + middle + late + second_row,
        first_row,
        trailing[0],
    )
    return (lower_first[None], lower_second[None], owned[None])


def solution(mesh):
    return jax.shard_map(
        functools.partial(per_device, mesh.shape["row"], mesh.shape["col"]),
        mesh=mesh,
        in_specs=(
            P(("row", "col"), None, None),
            P(("row", "col"), None, None),
            P("col", None),
            P("col", None),
            P("col", None),
            P(("row", "col"), None, None, None),
            P(("row", "col"), None, None),
            P(("row", "col")),
        ),
        out_specs=(
            P(("row", "col"), None, None),
            P(("row", "col"), None, None),
            P(("row", "col"), None, None, None),
        ),
        check_vma=False,
    )
```
